512 devices in a mesh: seq: 64 (over y, z), head: 8 (over x, core).
Axes of the slice: x: 4, y: 4, z: 16, core: 2. Of those that a mesh axis runs over, the one named last changes fastest.
Arguments:
- queries: bfloat16 [65536, 4096], P('seq', 'head'), may hold values from -6 to 6
- keys: bfloat16 [65536, 4096], P('seq', 'head'), may hold values from -6 to 6
- values: bfloat16 [65536, 4096], P('seq', 'head'), may hold values from -6 to 6
- decay_rate: float32 [65536, 32], P('seq', 'head'), may hold values from 0 to 0.5
- gain: float32 [4096], replicated, may hold values from 0.25 to 1.75
Outputs:
- normed: bfloat16 [65536, 4096], P(('seq', 'head'))
The draws below stay inside these ranges and needn't reach their ends.
All inputs are finite; a program needn't handle non-finite values. Where the reference program divides by a largest or mean magnitude, that divisor is 1e-20 or more.
Results may differ from the reference program's by a relative error of at most 0.017.
Values may be sent and summed in bfloat16 or wider, within the bound.
No kernel may reach another device: no remote copies, remote signals or barrier semaphores. Data moves between devices by JAX's collectives and lax.ppermute only.
A program may use at most 64 MiB of HBM per device.

```python
import math
import jax
import jax.numpy as jnp
from jax import lax

HEADS = 32
DK = 128
TOK_DEV = 1024
SEQUENCE_TOKENS = 65536
D_MODEL = 4096
N_SEQ = 64


def draw_decay_rate(key, part):
    key = jax.random.fold_in(key, 11)
    selection_random_key, quick_random_key, gradual_random_key, coarse_random_key, spike_random_key, penalty_random_key = jax.random.split(key, 6)
    fast_share = 0.4
    picked = jax.random.uniform(selection_random_key, (HEADS,), jnp.float32) < fast_share
    fast_rate = jax.random.uniform(quick_random_key, (HEADS,), jnp.float32, 1.0 / 50.0, 1.0 / 30.0)
    slow_rate = jnp.exp(jax.random.uniform(gradual_random_key, (HEADS,), jnp.float32, math.log(0.1), 0.0)) / SEQUENCE_TOKENS
    base_rate = jnp.where(picked, fast_rate, slow_rate)
    rough = jnp.exp(jax.random.uniform(coarse_random_key, (SEQUENCE_TOKENS, HEADS), jnp.float32, -math.log(2.0), math.log(2.0)))
    spike_position = jax.random.randint(spike_random_key, (2,), 0, SEQUENCE_TOKENS)
    spike_penalty = jax.random.uniform(penalty_random_key, (2,), jnp.float32, 0.2, 0.35)
    marked_locations = jnp.arange(SEQUENCE_TOKENS)[:, None] == spike_position[None, :]
    additional_term = jnp.sum(jnp.where(marked_locations, -jnp.log(1.0 - spike_penalty)[None, :], 0.0), axis=1)
    return base_rate[None, :] * rough + additional_term[:, None]


def shard_levels(stream_key, dims, cuts, low, top_value):
    def one(axis_at, shards_of):
        steps = jax.random.uniform(jax.random.fold_in(jax.random.fold_in(stream_key, 6), axis_at), (shards_of,), jnp.float32, low / len(cuts), top_value / len(cuts))
        return jnp.repeat(jnp.exp(steps), dims[axis_at] // shards_of).reshape((-1,) + (1,) * (len(dims) - axis_at - 1))

    level = one(*cuts[0])
    for cut in cuts[1:]:
        level = level * one(*cut)
    return level


def bell_draw(stream_key, shape, scale, reach, pieces=(), held_as=jnp.bfloat16):
    array = jax.random.normal(stream_key, shape, jnp.float32) * scale
    if len(pieces) > 0:
        array = shard_levels(stream_key, shape, pieces, -0.22, 0.18) * array
    return jnp.clip(array, min=-reach, max=reach).astype(held_as)


def setup_inputs(seed: int = 0) -> dict:
    streams_of = jax.random.split(jax.random.key(seed), 6)
    return {
        "queries": bell_draw(streams_of[0], (SEQUENCE_TOKENS, D_MODEL), 1.0, 6.0, ((0, 64), (1, 8))),
        "keys": bell_draw(streams_of[1], (SEQUENCE_TOKENS, D_MODEL), 1.0, 6.0, ((0, 64), (1, 8))),
        "values": bell_draw(streams_of[2], (SEQUENCE_TOKENS, D_MODEL), 1.0, 6.0, ((0, 64), (1, 8))),
        "decay_rate": draw_decay_rate(jax.random.fold_in(streams_of[5], 71), 0),
        "gain": jnp.clip(1.0 + 0.15 * jax.random.normal(streams_of[4], (D_MODEL,), jnp.float32), 0.25, 1.75),
    }


def reference(queries, keys, values, decay_rate, gain):
    inverse_root = DK ** (-0.5)
    query_grid = queries.reshape(N_SEQ, TOK_DEV, HEADS, DK)
    key_grid = keys.reshape(N_SEQ, TOK_DEV, HEADS, DK)
    value_grid = values.reshape(N_SEQ, TOK_DEV, HEADS, DK)
    rate_grid = decay_rate.reshape(N_SEQ, TOK_DEV, HEADS)
    positions = jnp.arange(TOK_DEV)
    causal = positions[:, None] >= positions[None, :]

    def shard_step(running, inputs):
        query_blk, key_blk, value_blk, rate_blk = inputs
        decayed = -jnp.cumsum(rate_blk, axis=0)
        incoming = running.astype(jnp.bfloat16)
        carried = jnp.einsum('thd,hde->the', query_blk.astype(jnp.float32), incoming.astype(jnp.float32))
        carried = carried * (jnp.exp(decayed) * inverse_root)[:, :, None]
        scores = jnp.einsum('thd,shd->hts', query_blk.astype(jnp.float32), key_blk.astype(jnp.float32))
        spread = decayed.T[:, :, None] - decayed.T[:, None, :]
        decay_mat = jnp.exp(jnp.where(causal[None], spread, -jnp.inf))
        weight = (scores * decay_mat * inverse_root).astype(jnp.bfloat16)
        within = jnp.einsum('hts,shd->thd', weight.astype(jnp.float32), value_blk.astype(jnp.float32))
        retained = (within + carried).astype(jnp.bfloat16)
        last_row = decayed[-1]
        decayed_keys = (key_blk.astype(jnp.float32) * jnp.exp(last_row[None, :] - decayed)[:, :, None]).astype(jnp.bfloat16)
        summary = jnp.einsum('shd,she->hde', decayed_keys.astype(jnp.float32), value_blk.astype(jnp.float32))
        scales = (lax.optimization_barrier(jnp.max(jnp.abs(summary), axis=2)) + 1e-06).astype(jnp.bfloat16).astype(jnp.float32)
        code_words = (summary / scales[:, :, None]).astype(jnp.bfloat16)
        restored = code_words.astype(jnp.float32) * scales[:, :, None]
        updated = jnp.exp(last_row)[:, None, None] * running + restored
        return (updated, retained)
    start_state = jnp.zeros((HEADS, DK, DK), jnp.float32)
    final_state, retained = lax.scan(shard_step, start_state, (query_grid, key_grid, value_grid, rate_grid))
    flat = retained.reshape(SEQUENCE_TOKENS, HEADS, DK).astype(jnp.float32)
    center = lax.optimization_barrier(jnp.mean(flat, axis=2, keepdims=True))
    deviation = flat - center
    variance = lax.optimization_barrier(jnp.mean(deviation * deviation, axis=2, keepdims=True))
    normed = deviation / jnp.sqrt(variance + 1e-05) * gain.reshape(HEADS, DK)[None]
    return normed.astype(jnp.bfloat16).reshape(SEQUENCE_TOKENS, HEADS * DK)
```

```python
import functools

import jax
import jax.numpy as jnp
from jax import lax
from jax.experimental import pallas as pl
from jax.experimental.pallas import tpu as pltpu
from jax.sharding import PartitionSpec as P

LANE = 128
F32 = jnp.float32
BF16 = jnp.bfloat16
VMEM_BYTES = 48 * 1024 * 1024


def split_three(x):
    high = x.astype(BF16)
    rest = x - high.astype(F32)
    middle = rest.astype(BF16)
    low = (rest - middle.astype(F32)).astype(BF16)
    return high, middle, low


def chunk_sums(rate_row, after):
    tokens = rate_row.shape[1]
    count = tokens // LANE
    rows = jnp.concatenate([rate_row[:, n * LANE : (n + 1) * LANE] for n in range(count)], axis=0)
    source = lax.broadcasted_iota(jnp.int32, (LANE, LANE), 0)
    target = lax.broadcasted_iota(jnp.int32, (LANE, LANE), 1)
    picked = (source > target) if after else (source <= target)
    picked = jnp.where(picked, 1.0, 0.0).astype(BF16)
    sums = sum(jnp.dot(part, picked, preferred_element_type=F32) for part in split_three(rows))
    if after:
        totals = sums[:, :1] + rows[:, :1]
    else:
        totals = sums[:, LANE - 1 :]
    running = jnp.zeros((1, 1), F32)
    pieces = [None] * count
    for n in reversed(range(count)) if after else range(count):
        pieces[n] = sums[n : n + 1] + running
        running = running + totals[n : n + 1]
    return pieces, running


def summary_kernel(rate_ref, key_ref, value_ref, out_ref):
    head = pl.program_id(0)
    later, total = chunk_sums(rate_ref[pl.ds(head, 1), :], after=True)
    decay = jnp.exp(-jnp.concatenate(later, axis=1))
    key_t = key_ref[...].T
    decayed_keys = (key_t.astype(F32) * decay).astype(BF16)
    summary = jnp.dot(decayed_keys, value_ref[...], preferred_element_type=F32)
    size = summary.shape[0]
    scales = (jnp.max(jnp.abs(summary), axis=1, keepdims=True) + 1e-06).astype(BF16).astype(F32)
    codes = (summary / scales).astype(BF16)
    restored = (codes.astype(F32) * scales).astype(BF16)
    keep = jnp.broadcast_to(jnp.exp(-total), (1, LANE))
    parts = jnp.concatenate([p.astype(F32) for p in split_three(keep)] + [jnp.zeros((5, LANE), F32)], axis=0)
    parts = parts.astype(BF16)
    out_ref[:, :8, :] = restored.reshape(size // 8, 8, LANE)
    out_ref[:, 8:, :] = jnp.broadcast_to(parts[None], (size // 8, 8, LANE))


def scan_kernel(in_ref, out_ref):
    blocks = in_ref.shape[0]

    def step(i, state):
        out_ref[i] = state.astype(BF16)
        block = in_ref[i].astype(F32)
        keep = block[8:9] + block[9:10] + block[10:11]
        return state * keep + block[:8]

    lax.fori_loop(0, blocks, step, jnp.zeros((8, LANE), F32), unroll=4)


def within_kernel(inverse_root, span, rate_ref, query_ref, key_ref, value_ref, within_ref, query_out_ref):
    head = pl.program_id(0)
    tokens = query_ref.shape[0]
    upto, _ = chunk_sums(rate_ref[pl.ds(head, 1), :], after=False)
    count = len(upto)
    stacked = -jnp.concatenate(upto, axis=0)
    columns = jnp.concatenate([stacked] * (LANE // count), axis=0).T
    column = jnp.concatenate([columns[:, n : n + 1] for n in range(count)], axis=0)
    row = -jnp.concatenate(upto, axis=1)
    query = query_ref[...]
    query_out_ref[...] = (query.astype(F32) * (jnp.exp(column) * inverse_root)).astype(BF16)
    place_t = lax.broadcasted_iota(jnp.int32, (span, span), 0)
    place_s = lax.broadcasted_iota(jnp.int32, (span, span), 1)
    for i in range(tokens // span):
        at_t = slice(i * span, (i + 1) * span)
        total = jnp.zeros((span, query.shape[1]), F32)
        for j in range(i + 1):
            at_s = slice(j * span, (j + 1) * span)
            scores = lax.dot_general(
                query[at_t], key_ref[at_s, :], (((1,), (1,)), ((), ())), preferred_element_type=F32
            )
            spread = column[at_t] - row[:, at_s]
            if i == j:
                spread = jnp.where(place_t >= place_s, spread, -jnp.inf)
            weight = (scores * jnp.exp(spread) * inverse_root).astype(BF16)
            total += jnp.dot(weight, value_ref[at_s, :], preferred_element_type=F32)
        within_ref[at_t, :] = total


def finish_kernel(query_ref, within_ref, incoming_ref, gain_ref, out_ref):
    carried = jnp.dot(query_ref[...], incoming_ref[0], preferred_element_type=F32)
    retained = (within_ref[...] + carried).astype(BF16)
    size = retained.shape[1]
    ones = jnp.ones((size, size), BF16)
    center = jnp.dot(retained, ones, preferred_element_type=F32) * (1.0 / size)
    deviation = retained.astype(F32) - center
    square = deviation * deviation
    high = square.astype(BF16)
    low = (square - high.astype(F32)).astype(BF16)
    variance = jnp.dot(high, ones, preferred_element_type=F32) + jnp.dot(low, ones, preferred_element_type=F32)
    variance = variance * (1.0 / size)
    out_ref[...] = (deviation * lax.rsqrt(variance + 1e-05) * gain_ref[...]).astype(BF16)


def per_device(queries, keys, values, decay_rate, gain):
    tokens, features = queries.shape
    heads = decay_rate.shape[1]
    size = features // heads
    inverse_root = size ** (-0.5)
    blocks = lax.axis_size("seq")
    owners = lax.axis_size("head")
    rates = decay_rate.T
    params = pltpu.CompilerParams(vmem_limit_bytes=VMEM_BYTES)
    tall = pl.BlockSpec((tokens, size), lambda h: (0, h))
    whole_rates = pl.BlockSpec((heads, tokens), lambda h: (0, 0))
    state_rows = heads * size // blocks

    with jax.named_scope("summaries"):
        payload = pl.pallas_call(
            summary_kernel,
            grid=(heads,),
            in_specs=[whole_rates, tall, tall],
            out_specs=pl.BlockSpec((size // 8, 16, size), lambda h: (h, 0, 0)),
            out_shape=jax.ShapeDtypeStruct((blocks, 16, size), BF16),
            compiler_params=params,
            cost_estimate=pl.CostEstimate(flops=2 * heads * tokens * size * size, bytes_accessed=4 * tokens * features, transcendentals=0),
        )(rates, keys, values)
    gathered = lax.all_to_all(payload, "seq", 0, 0, tiled=True)
    with jax.named_scope("within"):
        within, scaled_queries = pl.pallas_call(
            functools.partial(within_kernel, inverse_root, 256),
            grid=(heads,),
            in_specs=[whole_rates, tall, tall, tall],
            out_specs=[tall, tall],
            out_shape=[
                jax.ShapeDtypeStruct((tokens, features), F32),
                jax.ShapeDtypeStruct((tokens, features), BF16),
            ],
            compiler_params=params,
            cost_estimate=pl.CostEstimate(
                flops=3 * heads * tokens * tokens * size, bytes_accessed=12 * tokens * features, transcendentals=heads * tokens * tokens
            ),
        )(rates, queries, keys, values)
    with jax.named_scope("block_scan"):
        before = pl.pallas_call(
            scan_kernel,
            out_shape=jax.ShapeDtypeStruct((blocks, 8, size), BF16),
            compiler_params=params,
        )(gathered)
    incoming = lax.all_to_all(before, "seq", 0, 0, tiled=True).reshape(heads, size, size)
    my_gain = lax.dynamic_slice_in_dim(gain, lax.axis_index("head") * features, features)[None]
    with jax.named_scope("finish"):
        normed = pl.pallas_call(
            finish_kernel,
            grid=(heads,),
            in_specs=[
                tall,
                tall,
                pl.BlockSpec((1, size, size), lambda h: (h, 0, 0)),
                pl.BlockSpec((1, size), lambda h: (0, h)),
            ],
            out_specs=tall,
            out_shape=jax.ShapeDtypeStruct((tokens, features), BF16),
            compiler_params=params,
        )(scaled_queries, within, incoming, my_gain)
    sent = normed.reshape(owners, tokens // owners, features)
    got = lax.all_to_all(sent, "head", 0, 0, tiled=True)
    return got.transpose(1, 0, 2).reshape(tokens // owners, owners * features)


def solution(mesh):
    placed = (P("seq", "head"), P("seq", "head"), P("seq", "head"), P("seq", "head"), P())
    return jax.shard_map(
        per_device, mesh=mesh, in_specs=placed, out_specs=P(("seq", "head"), None), check_vma=False
    )
```

```python
import functools
import math

import jax
import jax.numpy as jnp
from jax import lax
from jax.experimental import pallas as pl
from jax.experimental.pallas import tpu as pltpu
from jax.sharding import PartitionSpec as P

LANE = 128
F32 = jnp.float32
BF16 = jnp.bfloat16
SLOT = 10
LOG2_E = 1.4426950408889634
SMALL_VMEM = 16 * 1024 * 1024
LARGE_VMEM = 40 * 1024 * 1024


def split_three(x):
    high = x.astype(BF16)
    rest = x - high.astype(F32)
    middle = rest.astype(BF16)
    low = (rest - middle.astype(F32)).astype(BF16)
    return high, middle, low


def chunk_sums(rates, after):
    heads, tokens = rates.shape
    count = tokens // LANE
    rows = jnp.concatenate([rates[:, n * LANE : (n + 1) * LANE] for n in range(count)], axis=0)
    source = lax.broadcasted_iota(jnp.int32, (LANE, LANE), 0)
    target = lax.broadcasted_iota(jnp.int32, (LANE, LANE), 1)
    picked = (source > target) if after else (source <= target)
    picked = jnp.where(picked, 1.0, 0.0).astype(BF16)
    sums = sum(jnp.dot(part, picked, preferred_element_type=F32) for part in split_three(rows))
    if after:
        totals = sums[:, :1] + rows[:, :1]
    else:
        totals = sums[:, LANE - 1 :]
    running = jnp.zeros((heads, 1), F32)
    pieces = [None] * count
    for n in reversed(range(count)) if after else range(count):
        at = slice(n * heads, (n + 1) * heads)
        pieces[n] = sums[at] + running
        running = running + totals[at]
    return pieces, running


def summary_kernel(rate_hbm, key_hbm, value_hbm, out_ref, rates_ref, key_ref, value_ref, sems):
    heads, tokens = rates_ref.shape
    size = key_ref.shape[1] // heads
    copies = [
        pltpu.make_async_copy(source, target, sems.at[n])
        for n, (source, target) in enumerate(
            ((rate_hbm, rates_ref), (key_hbm, key_ref), (value_hbm, value_ref))
        )
    ]
    for copy in copies:
        copy.start()
    copies[0].wait()
    later, totals = chunk_sums(rates_ref[...], after=True)
    decays = jnp.exp(-jnp.concatenate(later, axis=1))
    keeps = jnp.exp(-totals)
    copies[1].wait()
    decayed_keys = []
    for h in range(heads):
        key_t = key_ref[:, h * size : (h + 1) * size].T
        decayed_keys.append((key_t.astype(F32) * decays[h : h + 1]).astype(BF16))
    copies[2].wait()
    for h in range(heads):
        summary = jnp.dot(decayed_keys[h], value_ref[:, h * size : (h + 1) * size], preferred_element_type=F32)
        scales = (jnp.max(jnp.abs(summary), axis=1, keepdims=True) + 1e-06).astype(BF16).astype(F32)
        codes = (summary / scales).astype(BF16)
        restored = codes.astype(F32) * scales
        keep = jnp.broadcast_to(keeps[h : h + 1], (1, LANE))
        parts = [p.astype(F32) for p in split_three(keep)[:2]]
        rows = []
        for i in range(size // 8):
            rows += [restored[i * 8 : (i + 1) * 8]] + parts
        filled = size // 8 * SLOT
        out_ref[h * filled : (h + 1) * filled, :] = jnp.concatenate(rows, axis=0).astype(BF16)


def scan_kernel(in_ref, out_ref):
    blocks = out_ref.shape[0]
    state = jnp.zeros((8, LANE), F32)
    for first in range(0, blocks, 8):
        rows = in_ref[first * SLOT : (first + 8) * SLOT, :].astype(F32)
        states = []
        for i in range(8):
            states.append(state)
            slot = rows[i * SLOT : (i + 1) * SLOT]
            state = state * (slot[8:9] + slot[9:10]) + slot[:8]
        out_ref[first : first + 8] = jnp.stack(states).astype(BF16)


def within_kernel(
    span,
    head_group_ref,
    gain_ref,
    rate_hbm,
    query_hbm,
    key_hbm,
    value_hbm,
    parts_ref,
    gain_out_ref,
    rates_ref,
    inputs_ref,
    total_ref,
    sems,
):
    heads, tokens = rates_ref.shape
    size = inputs_ref.shape[3]
    rate_copy = pltpu.make_async_copy(rate_hbm, rates_ref, sems.at[0])
    rate_copy.start()
    copies = []
    for h in range(heads):
        for n, source in enumerate((query_hbm, key_hbm, value_hbm)):
            copy = pltpu.make_async_copy(
                source.at[:, pl.ds(h * size, size)], inputs_ref.at[h, n], sems.at[1 + 3 * h + n]
            )
            copy.start()
            copies.append(copy)
    for h in range(heads):
        gain_out_ref[h : h + 1] = gain_ref[pl.ds(head_group_ref[0] * heads + h, 1), :]
    rate_copy.wait()
    upto, _ = chunk_sums(rates_ref[...], after=False)
    count = len(upto)
    stacked = -jnp.concatenate(upto, axis=0) * LOG2_E
    columns = jnp.concatenate([stacked] * (LANE // (count * heads)), axis=0).T
    place_t = lax.broadcasted_iota(jnp.int32, (span, span), 0)
    place_s = lax.broadcasted_iota(jnp.int32, (span, span), 1)
    for h in range(heads):
        for copy in copies[3 * h : 3 * h + 3]:
            copy.wait()
        at_h = slice(h * size, (h + 1) * size)
        places = [n * heads + h for n in range(count)]
        column = jnp.concatenate([columns[:, n : n + 1] for n in places], axis=0) - 0.5 * math.log2(size)
        row = jnp.concatenate([stacked[n : n + 1] for n in places], axis=1)
        parts_ref[0, :, at_h] = (inputs_ref[h, 0].astype(F32) * jnp.exp2(column)).astype(BF16)
        for first in range(0, tokens, span):
            at_s = slice(first, first + span)
            scores = lax.dot_general(
                inputs_ref[h, 0, first:, :],
                inputs_ref[h, 1, at_s, :],
                (((1,), (1,)), ((), ())),
                preferred_element_type=F32,
            )
            weights = []
            for start in range(first, tokens, span):
                spread = column[start : start + span] - row[:, at_s]
                if start == first:
                    spread = jnp.where(place_t >= place_s, spread, -jnp.inf)
                weights.append((scores[start - first : start - first + span] * jnp.exp2(spread)).astype(BF16))
            part = jnp.dot(jnp.concatenate(weights, axis=0), inputs_ref[h, 2, at_s, :], preferred_element_type=F32)
            if first == 0:
                total_ref[...] = part
            else:
                total_ref[first:, :] += part
        parts_ref[1, :, at_h] = total_ref[...].astype(BF16)


def finish_kernel(span, parts_ref, incoming_ref, gain_ref, out_ref):
    tokens = parts_ref.shape[1]
    heads, size, _ = incoming_ref.shape
    mean_of = jnp.full((size, size), 1.0 / size, BF16)
    for h in range(heads):
        columns = slice(h * size, (h + 1) * size)
        gain = gain_ref[h : h + 1]
        for first in range(0, tokens, span):
            at = slice(first, first + span)
            carried = jnp.dot(parts_ref[0, at, columns], incoming_ref[h], preferred_element_type=F32)
            retained = (parts_ref[1, at, columns].astype(F32) + carried).astype(BF16)
            center = jnp.dot(retained, mean_of, preferred_element_type=F32)
            deviation = retained.astype(F32) - center
            variance = jnp.sum(deviation * deviation, axis=1, keepdims=True) * (1.0 / size)
            out_ref[at, columns] = (deviation * lax.rsqrt(variance + 1e-05) * gain).astype(BF16)


def per_device(queries, keys, values, decay_rate, gain):
    tokens, features = queries.shape
    heads = decay_rate.shape[1]
    size = features // heads
    blocks = lax.axis_size("seq")
    owners = lax.axis_size("head")
    rates = decay_rate.T
    params = pltpu.CompilerParams(vmem_limit_bytes=SMALL_VMEM)

    in_hbm = pl.BlockSpec(memory_space=pl.ANY)
    in_vmem = pl.BlockSpec(memory_space=pltpu.VMEM)
    in_smem = pl.BlockSpec(memory_space=pltpu.SMEM)
    head_group = lax.axis_index("head").astype(jnp.int32).reshape(1)

    with jax.named_scope("summaries"):
        payload = pl.pallas_call(
            summary_kernel,
            in_specs=[in_hbm] * 3,
            out_specs=in_vmem,
            out_shape=jax.ShapeDtypeStruct((blocks * SLOT, size), BF16),
            scratch_shapes=[
                pltpu.VMEM((heads, tokens), F32),
                pltpu.VMEM((tokens, features), BF16),
                pltpu.VMEM((tokens, features), BF16),
                pltpu.SemaphoreType.DMA((3,)),
            ],
            cost_estimate=pl.CostEstimate(flops=2 * heads * tokens * size * size, bytes_accessed=4 * tokens * features, transcendentals=0),
        )(rates, keys, values)
    slots = payload.reshape(blocks, SLOT // 2, 2, size)
    gathered = lax.all_to_all(slots, "seq", 0, 0, tiled=True).reshape(blocks * SLOT, size)
    with jax.named_scope("within"):
        parts, my_gain = pl.pallas_call(
            functools.partial(within_kernel, 256),
            in_specs=[in_smem, in_vmem] + [in_hbm] * 4,
            out_specs=[in_vmem] * 2,
            out_shape=[
                jax.ShapeDtypeStruct((2, tokens, features), BF16),
                jax.ShapeDtypeStruct((heads, size), F32),
            ],
            scratch_shapes=[
                pltpu.VMEM((heads, tokens), F32),
                pltpu.VMEM((heads, 3, tokens, size), BF16),
                pltpu.VMEM((tokens, size), F32),
                pltpu.SemaphoreType.DMA((1 + 3 * heads,)),
            ],
            compiler_params=pltpu.CompilerParams(vmem_limit_bytes=LARGE_VMEM),
            cost_estimate=pl.CostEstimate(
                flops=3 * heads * tokens * tokens * size, bytes_accessed=12 * tokens * features, transcendentals=heads * tokens * tokens
            ),
        )(head_group, gain.reshape(-1, size), rates, queries, keys, values)
    gathered, parts, my_gain = lax.optimization_barrier((gathered, parts, my_gain))
    with jax.named_scope("block_scan"):
        before = pl.pallas_call(
            scan_kernel,
            in_specs=[in_vmem],
            out_specs=in_vmem,
            out_shape=jax.ShapeDtypeStruct((blocks, 8, size), BF16),
            compiler_params=params,
        )(gathered)
    incoming = lax.all_to_all(before, "seq", 0, 0, tiled=True).reshape(heads, size, size)
    with jax.named_scope("finish"):
        normed = pl.pallas_call(
            functools.partial(finish_kernel, 256),
            in_specs=[in_vmem] * 3,
            out_specs=in_vmem,
            out_shape=jax.ShapeDtypeStruct((tokens, features), BF16),
            compiler_params=params,
        )(parts, incoming, my_gain)
    sent = normed.reshape(owners, tokens // owners, features)
    got = lax.all_to_all(sent, "head", 0, 0, tiled=True)
    return got.transpose(1, 0, 2).reshape(tokens // owners, owners * features)


def solution(mesh):
    placed = (P("seq", "head"), P("seq", "head"), P("seq", "head"), P("seq", "head"), P())
    return jax.shard_map(
        per_device, mesh=mesh, in_specs=placed, out_specs=P(("seq", "head"), None), check_vma=False
    )
```

```python
import functools
import math

import jax
import jax.numpy as jnp
from jax import lax
from jax.experimental import pallas as pl
from jax.experimental.pallas import tpu as pltpu
from jax.sharding import PartitionSpec as P

LANE = 128
F32 = jnp.float32
BF16 = jnp.bfloat16
SLOT = 10
FIRST_SEQ = 41
FIRST_HEAD = 4
LOG2_E = 1.4426950408889634
SMALL_VMEM = 16 * 1024 * 1024
LARGE_VMEM = 40 * 1024 * 1024


def split_three(x):
    high = x.astype(BF16)
    rest = x - high.astype(F32)
    middle = rest.astype(BF16)
    low = (rest - middle.astype(F32)).astype(BF16)
    return high, middle, low


def chunk_sums(rates, after):
    heads, tokens = rates.shape
    count = tokens // LANE
    rows = jnp.concatenate([rates[:, n * LANE : (n + 1) * LANE] for n in range(count)], axis=0)
    source = lax.broadcasted_iota(jnp.int32, (LANE, LANE), 0)
    target = lax.broadcasted_iota(jnp.int32, (LANE, LANE), 1)
    picked = (source > target) if after else (source <= target)
    picked = jnp.where(picked, 1.0, 0.0).astype(BF16)
    sums = sum(jnp.dot(part, picked, preferred_element_type=F32) for part in split_three(rows))
    if after:
        totals = sums[:, :1] + rows[:, :1]
    else:
        totals = sums[:, LANE - 1 :]
    running = jnp.zeros((heads, 1), F32)
    pieces = [None] * count
    for n in reversed(range(count)) if after else range(count):
        at = slice(n * heads, (n + 1) * heads)
        pieces[n] = sums[at] + running
        running = running + totals[at]
    return pieces, running


def summary_kernel(rate_hbm, key_hbm, value_hbm, out_ref, rates_ref, key_ref, value_ref, sems):
    heads, tokens = rates_ref.shape
    size = key_ref.shape[1] // heads
    copies = [
        pltpu.make_async_copy(source, target, sems.at[n])
        for n, (source, target) in enumerate(
            ((rate_hbm, rates_ref), (key_hbm, key_ref), (value_hbm, value_ref))
        )
    ]
    for copy in copies:
        copy.start()
    copies[0].wait()
    later, totals = chunk_sums(rates_ref[...], after=True)
    decays = jnp.exp(-jnp.concatenate(later, axis=1))
    keeps = jnp.exp(-totals)
    copies[1].wait()
    decayed_keys = []
    for h in range(heads):
        key_t = key_ref[:, h * size : (h + 1) * size].T
        decayed_keys.append((key_t.astype(F32) * decays[h : h + 1]).astype(BF16))
    copies[2].wait()
    for h in range(heads):
        summary = jnp.dot(decayed_keys[h], value_ref[:, h * size : (h + 1) * size], preferred_element_type=F32)
        scales = (jnp.max(jnp.abs(summary), axis=1, keepdims=True) + 1e-06).astype(BF16).astype(F32)
        codes = (summary / scales).astype(BF16)
        restored = codes.astype(F32) * scales
        keep = jnp.broadcast_to(keeps[h : h + 1], (1, LANE))
        parts = [p.astype(F32) for p in split_three(keep)[:2]]
        chunks = size // 8
        for start in range(0, chunks, 8):
            rows = []
            for i in range(start, start + 8):
                rows += [restored[i * 8 : (i + 1) * 8]] + parts
            slot = h * chunks + start
            out_ref[slot * SLOT : (slot + 8) * SLOT, :] = jnp.concatenate(rows, axis=0).astype(BF16)


def scan_kernel(order, in_ref, out_ref):
    state = jnp.zeros((8, LANE), F32)
    groups = [in_ref[n * SLOT : (n + 8) * SLOT, :].astype(F32) for n in range(0, len(order), 8)]
    for block in range(len(order)):
        slot = order.index(block)
        out_ref[slot] = state.astype(BF16)
        rows = groups[slot // 8]
        at = slot % 8 * SLOT
        keep = rows[at + 8 : at + 9] + rows[at + 9 : at + 10]
        state = state * keep + rows[at : at + 8]


def within_kernel(
    span,
    head_group_ref,
    gain_ref,
    rates_ref,
    query_ref,
    key_ref,
    value_ref,
    parts_ref,
    gain_out_ref,
    total_ref,
):
    heads, tokens = rates_ref.shape
    size = query_ref.shape[1] // heads
    for h in range(heads):
        gain_out_ref[h : h + 1] = gain_ref[pl.ds(head_group_ref[0] * heads + h, 1), :]
    upto, _ = chunk_sums(rates_ref[...], after=False)
    count = len(upto)
    stacked = -jnp.concatenate(upto, axis=0) * LOG2_E
    columns = jnp.concatenate([stacked] * (LANE // (count * heads)), axis=0).T
    place_t = lax.broadcasted_iota(jnp.int32, (span, span), 0)
    place_s = lax.broadcasted_iota(jnp.int32, (span, span), 1)
    for h in range(heads):
        at_h = slice(h * size, (h + 1) * size)
        places = [n * heads + h for n in range(count)]
        column = jnp.concatenate([columns[:, n : n + 1] for n in places], axis=0) - 0.5 * math.log2(size)
        row = jnp.concatenate([stacked[n : n + 1] for n in places], axis=1)
        parts_ref[0, :, at_h] = (query_ref[:, at_h].astype(F32) * jnp.exp2(column)).astype(BF16)
        for first in range(0, tokens, span):
            at_s = slice(first, first + span)
            scores = lax.dot_general(
                query_ref[first:, at_h],
                key_ref[at_s, at_h],
                (((1,), (1,)), ((), ())),
                preferred_element_type=F32,
            )
            weights = []
            for start in range(first, tokens, span):
                spread = column[start : start + span] - row[:, at_s]
                if start == first:
                    spread = jnp.where(place_t >= place_s, spread, -jnp.inf)
                weights.append((scores[start - first : start - first + span] * jnp.exp2(spread)).astype(BF16))
            part = jnp.dot(jnp.concatenate(weights, axis=0), value_ref[at_s, at_h], preferred_element_type=F32)
            if first == 0:
                total_ref[...] = part
            else:
                total_ref[first:, :] += part
        parts_ref[1, :, at_h] = total_ref[...].astype(BF16)


def finish_kernel(span, first_row, parts_ref, incoming_ref, gain_ref, out_ref):
    tokens = parts_ref.shape[1]
    heads, size, _ = incoming_ref.shape
    mean_of = jnp.full((size, size), 1.0 / size, BF16)
    for h in range(heads):
        columns = slice(h * size, (h + 1) * size)
        gain = gain_ref[h : h + 1]
        for first in range(0, tokens, span):
            at = slice(first, first + span)
            carried = jnp.dot(parts_ref[0, at, columns], incoming_ref[h], preferred_element_type=F32)
            retained = (parts_ref[1, at, columns].astype(F32) + carried).astype(BF16)
            center = jnp.dot(retained, mean_of, preferred_element_type=F32)
            deviation = retained.astype(F32) - center
            variance = jnp.sum(deviation * deviation, axis=1, keepdims=True) * (1.0 / size)
            to = (first - first_row) % tokens
            out_ref[to : to + span, columns] = (deviation * lax.rsqrt(variance + 1e-05) * gain).astype(BF16)


def lay_out_kernel(first, in_ref, out_hbm, sems):
    owners, _, features = in_ref.shape
    copies = []
    for n in range(owners):
        columns = pl.ds((n + first) % owners * features, features)
        copies.append(pltpu.make_async_copy(in_ref.at[n], out_hbm.at[:, columns], sems.at[n]))
    for copy in copies:
        copy.start()
    for copy in copies:
        copy.wait()


def exchange(slots, axis, order):
    return lax.all_to_all(slots, axis, 0, 0, tiled=True, axis_index_groups=[order])


def per_device(queries, keys, values, decay_rate, gain):
    tokens, features = queries.shape
    heads = decay_rate.shape[1]
    size = features // heads
    blocks = lax.axis_size("seq")
    owners = lax.axis_size("head")
    rates = decay_rate.T
    params = pltpu.CompilerParams(vmem_limit_bytes=SMALL_VMEM)

    in_hbm = pl.BlockSpec(memory_space=pl.ANY)
    in_vmem = pl.BlockSpec(memory_space=pltpu.VMEM)
    in_smem = pl.BlockSpec(memory_space=pltpu.SMEM)
    head_group = lax.axis_index("head").astype(jnp.int32).reshape(1)

    with jax.named_scope("summaries"):
        payload = pl.pallas_call(
            summary_kernel,
            in_specs=[in_hbm] * 3,
            out_specs=in_vmem,
            out_shape=jax.ShapeDtypeStruct((blocks * SLOT, size), BF16),
            scratch_shapes=[
                pltpu.VMEM((heads, tokens), F32),
                pltpu.VMEM((tokens, features), BF16),
                pltpu.VMEM((tokens, features), BF16),
                pltpu.SemaphoreType.DMA((3,)),
            ],
            cost_estimate=pl.CostEstimate(flops=2 * heads * tokens * size * size, bytes_accessed=4 * tokens * features, transcendentals=0),
        )(rates, keys, values)
    seq_order = [(n + FIRST_SEQ) % blocks for n in range(blocks)]
    slots = payload.reshape(blocks, SLOT // 2, 2, size)
    gathered = exchange(slots, "seq", seq_order).reshape(blocks * SLOT, size)
    with jax.named_scope("within"):
        parts, my_gain = pl.pallas_call(
            functools.partial(within_kernel, 256),
            in_specs=[in_smem] + [in_vmem] * 5,
            out_specs=[in_vmem] * 2,
            out_shape=[
                jax.ShapeDtypeStruct((2, tokens, features), BF16),
                jax.ShapeDtypeStruct((heads, size), F32),
            ],
            scratch_shapes=[pltpu.VMEM((tokens, size), F32)],
            compiler_params=pltpu.CompilerParams(vmem_limit_bytes=LARGE_VMEM),
            cost_estimate=pl.CostEstimate(
                flops=3 * heads * tokens * tokens * size, bytes_accessed=12 * tokens * features, transcendentals=heads * tokens * tokens
            ),
        )(head_group, gain.reshape(-1, size), rates, queries, keys, values)
    gathered, parts, my_gain = lax.optimization_barrier((gathered, parts, my_gain))
    with jax.named_scope("block_scan"):
        before = pl.pallas_call(
            functools.partial(scan_kernel, seq_order),
            in_specs=[in_vmem],
            out_specs=in_vmem,
            out_shape=jax.ShapeDtypeStruct((blocks, 8, size), BF16),
            compiler_params=params,
        )(gathered)
    incoming = exchange(before, "seq", seq_order).reshape(heads, size, size)
    with jax.named_scope("finish"):
        normed = pl.pallas_call(
            functools.partial(finish_kernel, 256, FIRST_HEAD * (tokens // owners)),
            in_specs=[in_vmem] * 3,
            out_specs=in_vmem,
            out_shape=jax.ShapeDtypeStruct((tokens, features), BF16),
            compiler_params=params,
        )(parts, incoming, my_gain)
    sent = normed.reshape(owners, tokens // owners, features)
    got = exchange(sent, "head", [(n + FIRST_HEAD) % owners for n in range(owners)])
    with jax.named_scope("lay_out"):
        return pl.pallas_call(
            functools.partial(lay_out_kernel, FIRST_HEAD),
            in_specs=[in_vmem],
            out_specs=in_hbm,
            out_shape=jax.ShapeDtypeStruct((tokens // owners, owners * features), BF16),
            scratch_shapes=[pltpu.SemaphoreType.DMA((owners,))],
            compiler_params=params,
        )(got)


def solution(mesh):
    placed = (P("seq", "head"), P("seq", "head"), P("seq", "head"), P("seq", "head"), P())
    return jax.shard_map(
        per_device, mesh=mesh, in_specs=placed, out_specs=P(("seq", "head"), None), check_vma=False
    )
```

```python
import functools
import math

import jax
import jax.numpy as jnp
from jax import lax
from jax.experimental import pallas as pl
from jax.experimental.pallas import tpu as pltpu
from jax.sharding import PartitionSpec as P

LANE = 128
F32 = jnp.float32
BF16 = jnp.bfloat16
PARTS = 8
QUAD = 4
NEAR = [1, 2, 3, 0]
FAR = [2, 3, 1, 0]
ROWS = [2, 3, 1, 0]
FIRST_HEAD = 4
LOG2_E = 1.4426950408889634
SMALL_VMEM = 16 * 1024 * 1024
LARGE_VMEM = 40 * 1024 * 1024


def split_three(x):
    high = x.astype(BF16)
    rest = x - high.astype(F32)
    middle = rest.astype(BF16)
    low = (rest - middle.astype(F32)).astype(BF16)
    return high, middle, low


def chunk_sums(rates, after):
    heads, tokens = rates.shape
    count = tokens // LANE
    rows = jnp.concatenate([rates[:, n * LANE : (n + 1) * LANE] for n in range(count)], axis=0)
    source = lax.broadcasted_iota(jnp.int32, (LANE, LANE), 0)
    target = lax.broadcasted_iota(jnp.int32, (LANE, LANE), 1)
    picked = (source > target) if after else (source <= target)
    picked = jnp.where(picked, 1.0, 0.0).astype(BF16)
    sums = sum(jnp.dot(part, picked, preferred_element_type=F32) for part in split_three(rows))
    if after:
        totals = sums[:, :1] + rows[:, :1]
    else:
        totals = sums[:, LANE - 1 :]
    running = jnp.zeros((heads, 1), F32)
    pieces = [None] * count
    for n in reversed(range(count)) if after else range(count):
        at = slice(n * heads, (n + 1) * heads)
        pieces[n] = sums[at] + running
        running = running + totals[at]
    return pieces, running


def put_state(ref, at, state, keep):
    parts = [p.astype(F32) for p in split_three(keep)]
    parts.append(jnp.zeros((PARTS - len(parts), LANE), F32))
    ref[at] = jnp.concatenate([state] + parts, axis=0).astype(BF16)


def take_state(ref, at):
    rows = ref[at].astype(F32)
    size = rows.shape[0] - PARTS
    return rows[:size], rows[size : size + 1] + rows[size + 1 : size + 2] + rows[size + 2 : size + 3]


def summary_kernel(rate_hbm, key_hbm, value_hbm, out_ref, rates_ref, key_ref, value_ref, sems):
    heads, tokens = rates_ref.shape
    size = key_ref.shape[1] // heads
    copies = [
        pltpu.make_async_copy(source, target, sems.at[n])
        for n, (source, target) in enumerate(
            ((rate_hbm, rates_ref), (key_hbm, key_ref), (value_hbm, value_ref))
        )
    ]
    for copy in copies:
        copy.start()
    copies[0].wait()
    later, totals = chunk_sums(rates_ref[...], after=True)
    decays = jnp.exp(-jnp.concatenate(later, axis=1))
    keeps = jnp.exp(-totals)
    copies[1].wait()
    decayed_keys = []
    for h in range(heads):
        key_t = key_ref[:, h * size : (h + 1) * size].T
        decayed_keys.append((key_t.astype(F32) * decays[h : h + 1]).astype(BF16))
    copies[2].wait()
    for h in range(heads):
        summary = jnp.dot(decayed_keys[h], value_ref[:, h * size : (h + 1) * size], preferred_element_type=F32)
        scales = (jnp.max(jnp.abs(summary), axis=1, keepdims=True) + 1e-06).astype(BF16).astype(F32)
        codes = (summary / scales).astype(BF16)
        restored = codes.astype(F32) * scales
        keep = jnp.broadcast_to(keeps[h : h + 1], (1, LANE))
        slots = out_ref.shape[0] // heads
        part = size // slots
        for n in range(slots):
            put_state(out_ref, (h * slots + n,), restored[n * part : (n + 1) * part], keep)


def slot_of(row, near):
    return ROWS.index(row) * QUAD + NEAR.index(near)


def total_kernel(in_ref, out_ref):
    for row in range(QUAD):
        state, keep = take_state(in_ref, (slot_of(row, 0),))
        for near in range(1, QUAD):
            more, more_keep = take_state(in_ref, (slot_of(row, near),))
            state = state * more_keep + more
            keep = keep * more_keep
        for n in range(QUAD):
            put_state(out_ref, (n, row), state, keep)


def carry_kernel(place_ref, groups_ref, blocks_ref, out_ref):
    mine = place_ref[0] // QUAD % QUAD
    carry = jnp.zeros(out_ref.shape[1:], F32)
    for row in range(QUAD):
        start = carry
        for far in range(QUAD):
            start = jnp.where(mine == far, carry, start)
            state, keep = take_state(groups_ref, (FAR.index(far), row))
            carry = carry * keep + state
        for near in range(QUAD):
            slot = slot_of(row, near)
            out_ref[slot] = start.astype(BF16)
            state, keep = take_state(blocks_ref, (slot,))
            start = start * keep + state


def within_kernel(
    span,
    place_ref,
    gain_ref,
    rates_ref,
    query_ref,
    key_ref,
    value_ref,
    parts_ref,
    gain_out_ref,
    place_out_ref,
    total_ref,
):
    heads, tokens = rates_ref.shape
    size = query_ref.shape[1] // heads
    place_out_ref[0] = place_ref[1]
    for h in range(heads):
        gain_out_ref[h : h + 1] = gain_ref[pl.ds(place_ref[0] * heads + h, 1), :]
    upto, _ = chunk_sums(rates_ref[...], after=False)
    count = len(upto)
    stacked = -jnp.concatenate(upto, axis=0) * LOG2_E
    columns = jnp.concatenate([stacked] * (LANE // (count * heads)), axis=0).T
    place_t = lax.broadcasted_iota(jnp.int32, (span, span), 0)
    place_s = lax.broadcasted_iota(jnp.int32, (span, span), 1)
    for h in range(heads):
        at_h = slice(h * size, (h + 1) * size)
        places = [n * heads + h for n in range(count)]
        column = jnp.concatenate([columns[:, n : n + 1] for n in places], axis=0) - 0.5 * math.log2(size)
        row = jnp.concatenate([stacked[n : n + 1] for n in places], axis=1)
        parts_ref[0, :, at_h] = (query_ref[:, at_h].astype(F32) * jnp.exp2(column)).astype(BF16)
        for first in range(0, tokens, span):
            at_s = slice(first, first + span)
            scores = lax.dot_general(
                query_ref[first:, at_h],
                key_ref[at_s, at_h],
                (((1,), (1,)), ((), ())),
                preferred_element_type=F32,
            )
            weights = []
            for start in range(first, tokens, span):
                spread = column[start : start + span] - row[:, at_s]
                if start == first:
                    spread = jnp.where(place_t >= place_s, spread, -jnp.inf)
                weights.append((scores[start - first : start - first + span] * jnp.exp2(spread)).astype(BF16))
            part = jnp.dot(jnp.concatenate(weights, axis=0), value_ref[at_s, at_h], preferred_element_type=F32)
            if first == 0:
                total_ref[...] = part
            else:
                total_ref[first:, :] += part
        parts_ref[1, :, at_h] = total_ref[...].astype(BF16)


def finish_kernel(span, first_row, parts_ref, incoming_ref, gain_ref, out_ref):
    tokens = parts_ref.shape[1]
    heads, size, _ = incoming_ref.shape
    mean_of = jnp.full((size, size), 1.0 / size, BF16)
    for h in range(heads):
        columns = slice(h * size, (h + 1) * size)
        gain = gain_ref[h : h + 1]
        for first in range(0, tokens, span):
            at = slice(first, first + span)
            carried = jnp.dot(parts_ref[0, at, columns], incoming_ref[h], preferred_element_type=F32)
            retained = (parts_ref[1, at, columns].astype(F32) + carried).astype(BF16)
            center = jnp.dot(retained, mean_of, preferred_element_type=F32)
            deviation = retained.astype(F32) - center
            variance = jnp.sum(deviation * deviation, axis=1, keepdims=True) * (1.0 / size)
            to = (first - first_row) % tokens
            out_ref[to : to + span, columns] = (deviation * lax.rsqrt(variance + 1e-05) * gain).astype(BF16)


def lay_out_kernel(first, in_ref, out_hbm, sems):
    owners, _, features = in_ref.shape
    copies = []
    for n in range(owners):
        columns = pl.ds((n + first) % owners * features, features)
        copies.append(pltpu.make_async_copy(in_ref.at[n], out_hbm.at[:, columns], sems.at[n]))
    for copy in copies:
        copy.start()
    for copy in copies:
        copy.wait()


def near_groups():
    return [
        [(row * QUAD + far) * QUAD + near for row in ROWS for near in NEAR] for far in range(QUAD)
    ]


def far_groups():
    return [
        [(row * QUAD + far) * QUAD + near for far in FAR] for row in range(QUAD) for near in range(QUAD)
    ]


def per_device(queries, keys, values, decay_rate, gain):
    tokens, features = queries.shape
    heads = decay_rate.shape[1]
    size = features // heads
    blocks = lax.axis_size("seq")
    owners = lax.axis_size("head")
    rates = decay_rate.T
    params = pltpu.CompilerParams(vmem_limit_bytes=SMALL_VMEM)

    in_hbm = pl.BlockSpec(memory_space=pl.ANY)
    in_vmem = pl.BlockSpec(memory_space=pltpu.VMEM)
    in_smem = pl.BlockSpec(memory_space=pltpu.SMEM)
    place = jnp.stack([lax.axis_index("head"), lax.axis_index("seq")]).astype(jnp.int32)
    part = heads * size // QUAD**2
    block_shape = jax.ShapeDtypeStruct((QUAD**2, part + PARTS, size), BF16)
    group_shape = jax.ShapeDtypeStruct((QUAD, QUAD, part + PARTS, size), BF16)

    def swap(sent, groups):
        return lax.all_to_all(sent, "seq", 0, 0, tiled=True, axis_index_groups=groups)

    with jax.named_scope("summaries"):
        payload = pl.pallas_call(
            summary_kernel,
            in_specs=[in_hbm] * 3,
            out_specs=in_vmem,
            out_shape=block_shape,
            scratch_shapes=[
                pltpu.VMEM((heads, tokens), F32),
                pltpu.VMEM((tokens, features), BF16),
                pltpu.VMEM((tokens, features), BF16),
                pltpu.SemaphoreType.DMA((3,)),
            ],
            cost_estimate=pl.CostEstimate(flops=2 * heads * tokens * size * size, bytes_accessed=4 * tokens * features, transcendentals=0),
        )(rates, keys, values)
    block_states = swap(payload, near_groups())
    with jax.named_scope("group_totals"):
        group_totals = pl.pallas_call(
            total_kernel, in_specs=[in_vmem], out_specs=in_vmem, out_shape=group_shape, compiler_params=params
        )(block_states)
    group_states = swap(group_totals, far_groups())
    block_states, late_rates = lax.optimization_barrier((block_states, rates))
    with jax.named_scope("within"):
        parts, my_gain, my_place = pl.pallas_call(
            functools.partial(within_kernel, 256),
            in_specs=[in_smem] + [in_vmem] * 5,
            out_specs=[in_vmem] * 2 + [in_smem],
            out_shape=[
                jax.ShapeDtypeStruct((2, tokens, features), BF16),
                jax.ShapeDtypeStruct((heads, size), F32),
                jax.ShapeDtypeStruct((1,), jnp.int32),
            ],
            scratch_shapes=[pltpu.VMEM((tokens, size), F32)],
            compiler_params=pltpu.CompilerParams(vmem_limit_bytes=LARGE_VMEM),
            cost_estimate=pl.CostEstimate(
                flops=3 * heads * tokens * tokens * size, bytes_accessed=12 * tokens * features, transcendentals=heads * tokens * tokens
            ),
        )(place, gain.reshape(-1, size), late_rates, queries, keys, values)
    group_states, parts, my_gain, my_place = lax.optimization_barrier((group_states, parts, my_gain, my_place))
    with jax.named_scope("carry"):
        before = pl.pallas_call(
            carry_kernel,
            in_specs=[in_smem] + [in_vmem] * 2,
            out_specs=in_vmem,
            out_shape=jax.ShapeDtypeStruct((QUAD**2, part, size), BF16),
            compiler_params=params,
        )(my_place, group_states, block_states)
    incoming = swap(before, near_groups()).reshape(heads, size, size)
    with jax.named_scope("finish"):
        normed = pl.pallas_call(
            functools.partial(finish_kernel, 256, FIRST_HEAD * (tokens // owners)),
            in_specs=[in_vmem] * 3,
            out_specs=in_vmem,
            out_shape=jax.ShapeDtypeStruct((tokens, features), BF16),
            compiler_params=params,
        )(parts, incoming, my_gain)
    sent = normed.reshape(owners, tokens // owners, features)
    head_order = [(n + FIRST_HEAD) % owners for n in range(owners)]
    got = lax.all_to_all(sent, "head", 0, 0, tiled=True, axis_index_groups=[head_order])
    with jax.named_scope("lay_out"):
        return pl.pallas_call(
            functools.partial(lay_out_kernel, FIRST_HEAD),
            in_specs=[in_vmem],
            out_specs=in_hbm,
            out_shape=jax.ShapeDtypeStruct((tokens // owners, owners * features), BF16),
            scratch_shapes=[pltpu.SemaphoreType.DMA((owners,))],
            compiler_params=params,
        )(got)


def solution(mesh):
    placed = (P("seq", "head"), P("seq", "head"), P("seq", "head"), P("seq", "head"), P())
    return jax.shard_map(
        per_device, mesh=mesh, in_specs=placed, out_specs=P(("seq", "head"), None), check_vma=False
    )
```

```python
import functools
import math

import jax
import jax.numpy as jnp
from jax import lax
from jax.experimental import pallas as pl
from jax.experimental.pallas import tpu as pltpu
from jax.sharding import PartitionSpec as P

LANE = 128
F32 = jnp.float32
BF16 = jnp.bfloat16
PARTS = 2
QUAD = 4
NEAR = [1, 2, 3, 0]
FAR = [2, 3, 1, 0]
ROWS = [2, 3, 1, 0]
FIRST_HEAD = 4
LOG2_E = 1.4426950408889634
SMALL_VMEM = 16 * 1024 * 1024
LARGE_VMEM = 40 * 1024 * 1024


def split_three(x):
    high = x.astype(BF16)
    rest = x - high.astype(F32)
    middle = rest.astype(BF16)
    low = (rest - middle.astype(F32)).astype(BF16)
    return high, middle, low


def chunk_sums(rates, after):
    heads, tokens = rates.shape
    count = tokens // LANE
    rows = jnp.concatenate([rates[:, n * LANE : (n + 1) * LANE] for n in range(count)], axis=0)
    source = lax.broadcasted_iota(jnp.int32, (LANE, LANE), 0)
    target = lax.broadcasted_iota(jnp.int32, (LANE, LANE), 1)
    picked = (source > target) if after else (source <= target)
    picked = jnp.where(picked, 1.0, 0.0).astype(BF16)
    sums = sum(jnp.dot(part, picked, preferred_element_type=F32) for part in split_three(rows))
    if after:
        totals = sums[:, :1] + rows[:, :1]
    else:
        totals = sums[:, LANE - 1 :]
    running = jnp.zeros((heads, 1), F32)
    pieces = [None] * count
    for n in reversed(range(count)) if after else range(count):
        at = slice(n * heads, (n + 1) * heads)
        pieces[n] = sums[at] + running
        running = running + totals[at]
    return pieces, running


def pack_states(states):
    rows = []
    for state, keep in states:
        rows += [state] + [p.astype(F32) for p in split_three(keep)[:PARTS]]
    return jnp.concatenate(rows, axis=0).astype(BF16)


def unpack_states(ref):
    half = ref.shape[0] // 2
    slot = ref.shape[0] // QUAD**2
    states = []
    for first in (0, half):
        rows = ref[first : first + half, :].astype(F32)
        for at in range(0, half, slot):
            keep = rows[at + slot - 2 : at + slot - 1] + rows[at + slot - 1 : at + slot]
            states.append((rows[at : at + slot - PARTS], keep))
    return states


def summary_kernel(rate_hbm, key_hbm, value_hbm, out_ref, rates_ref, key_ref, value_ref, sems):
    heads, tokens = rates_ref.shape
    size = key_ref.shape[1] // heads
    copies = [
        pltpu.make_async_copy(source, target, sems.at[n])
        for n, (source, target) in enumerate(
            ((rate_hbm, rates_ref), (key_hbm, key_ref), (value_hbm, value_ref))
        )
    ]
    for copy in copies:
        copy.start()
    copies[0].wait()
    later, totals = chunk_sums(rates_ref[...], after=True)
    decays = jnp.exp(-jnp.concatenate(later, axis=1))
    keeps = jnp.exp(-totals)
    copies[1].wait()
    decayed_keys = []
    for h in range(heads):
        key_t = key_ref[:, h * size : (h + 1) * size].T
        decayed_keys.append((key_t.astype(F32) * decays[h : h + 1]).astype(BF16))
    copies[2].wait()
    states = []
    for h in range(heads):
        summary = jnp.dot(decayed_keys[h], value_ref[:, h * size : (h + 1) * size], preferred_element_type=F32)
        scales = (jnp.max(jnp.abs(summary), axis=1, keepdims=True) + 1e-06).astype(BF16).astype(F32)
        codes = (summary / scales).astype(BF16)
        restored = codes.astype(F32) * scales
        keep = jnp.broadcast_to(keeps[h : h + 1], (1, LANE))
        part = heads * size // QUAD**2
        states += [(restored[n : n + part], keep) for n in range(0, size, part)]
    half = out_ref.shape[0] // 2
    for n in range(2):
        out_ref[n * half : (n + 1) * half, :] = pack_states(states[n * len(states) // 2 : (n + 1) * len(states) // 2])


def slot_of(row, near):
    return ROWS.index(row) * QUAD + NEAR.index(near)


def total_kernel(in_ref, out_ref):
    blocks = unpack_states(in_ref)
    totals = []
    for row in range(QUAD):
        state, keep = blocks[slot_of(row, 0)]
        for near in range(1, QUAD):
            more, more_keep = blocks[slot_of(row, near)]
            state = state * more_keep + more
            keep = keep * more_keep
        totals.append((state, keep))
    packed = pack_states(totals + totals)
    half = out_ref.shape[0] // 2
    for n in range(2):
        out_ref[n * half : (n + 1) * half, :] = packed


def carry_kernel(place_ref, groups_ref, blocks_ref, out_ref):
    groups, blocks = unpack_states(groups_ref), unpack_states(blocks_ref)
    mine = place_ref[0] // QUAD % QUAD
    carry = jnp.zeros(out_ref.shape[1:], F32)
    for row in range(QUAD):
        start = carry
        for far in range(QUAD):
            start = jnp.where(mine == far, carry, start)
            state, keep = groups[FAR.index(far) * QUAD + row]
            carry = carry * keep + state
        for near in range(QUAD):
            slot = slot_of(row, near)
            out_ref[slot] = start.astype(BF16)
            state, keep = blocks[slot]
            start = start * keep + state


def within_kernel(
    span,
    place_ref,
    gain_ref,
    rates_ref,
    query_ref,
    key_ref,
    value_ref,
    parts_ref,
    gain_out_ref,
    place_out_ref,
    total_ref,
):
    heads, tokens = rates_ref.shape
    size = query_ref.shape[1] // heads
    place_out_ref[0] = place_ref[1]
    for h in range(heads):
        gain_out_ref[h : h + 1] = gain_ref[pl.ds(place_ref[0] * heads + h, 1), :]
    upto, _ = chunk_sums(rates_ref[...], after=False)
    count = len(upto)
    stacked = -jnp.concatenate(upto, axis=0) * LOG2_E
    columns = jnp.concatenate([stacked] * (LANE // (count * heads)), axis=0).T
    place_t = lax.broadcasted_iota(jnp.int32, (span, span), 0)
    place_s = lax.broadcasted_iota(jnp.int32, (span, span), 1)
    for h in range(heads):
        at_h = slice(h * size, (h + 1) * size)
        places = [n * heads + h for n in range(count)]
        column = jnp.concatenate([columns[:, n : n + 1] for n in places], axis=0) - 0.5 * math.log2(size)
        row = jnp.concatenate([stacked[n : n + 1] for n in places], axis=1)
        parts_ref[0, :, at_h] = (query_ref[:, at_h].astype(F32) * jnp.exp2(column)).astype(BF16)
        for first in range(0, tokens, span):
            at_s = slice(first, first + span)
            scores = lax.dot_general(
                query_ref[first:, at_h],
                key_ref[at_s, at_h],
                (((1,), (1,)), ((), ())),
                preferred_element_type=F32,
            )
            weights = []
            for start in range(first, tokens, span):
                spread = column[start : start + span] - row[:, at_s]
                if start == first:
                    spread = jnp.where(place_t >= place_s, spread, -jnp.inf)
                weights.append((scores[start - first : start - first + span] * jnp.exp2(spread)).astype(BF16))
            part = jnp.dot(jnp.concatenate(weights, axis=0), value_ref[at_s, at_h], preferred_element_type=F32)
            if first == 0:
                total_ref[...] = part
            else:
                total_ref[first:, :] += part
        parts_ref[1, :, at_h] = total_ref[...].astype(BF16)


def finish_kernel(span, first_row, parts_ref, incoming_ref, gain_ref, out_ref):
    tokens = parts_ref.shape[1]
    heads, size, _ = incoming_ref.shape
    mean_of = jnp.full((size, size), 1.0 / size, BF16)
    for h in range(heads):
        columns = slice(h * size, (h + 1) * size)
        gain = gain_ref[h : h + 1]
        for first in range(0, tokens, span):
            at = slice(first, first + span)
            carried = jnp.dot(parts_ref[0, at, columns], incoming_ref[h], preferred_element_type=F32)
            retained = (parts_ref[1, at, columns].astype(F32) + carried).astype(BF16)
            center = jnp.dot(retained, mean_of, preferred_element_type=F32)
            deviation = retained.astype(F32) - center
            variance = jnp.sum(deviation * deviation, axis=1, keepdims=True) * (1.0 / size)
            to = (first - first_row) % tokens
            out_ref[to : to + span, columns] = (deviation * lax.rsqrt(variance + 1e-05) * gain).astype(BF16)


def lay_out_kernel(first, in_ref, out_hbm, sems):
    owners, _, features = in_ref.shape
    copies = []
    for n in range(owners):
        columns = pl.ds((n + first) % owners * features, features)
        copies.append(pltpu.make_async_copy(in_ref.at[n], out_hbm.at[:, columns], sems.at[n]))
    for copy in copies:
        copy.start()
    for copy in copies:
        copy.wait()


def near_groups():
    return [
        [(row * QUAD + far) * QUAD + near for row in ROWS for near in NEAR] for far in range(QUAD)
    ]


def far_groups():
    return [
        [(row * QUAD + far) * QUAD + near for far in FAR] for row in range(QUAD) for near in range(QUAD)
    ]


def per_device(queries, keys, values, decay_rate, gain):
    tokens, features = queries.shape
    heads = decay_rate.shape[1]
    size = features // heads
    blocks = lax.axis_size("seq")
    owners = lax.axis_size("head")
    rates = decay_rate.T
    params = pltpu.CompilerParams(vmem_limit_bytes=SMALL_VMEM)

    in_hbm = pl.BlockSpec(memory_space=pl.ANY)
    in_vmem = pl.BlockSpec(memory_space=pltpu.VMEM)
    in_smem = pl.BlockSpec(memory_space=pltpu.SMEM)
    place = jnp.stack([lax.axis_index("head"), lax.axis_index("seq")]).astype(jnp.int32)
    part = heads * size // QUAD**2
    state_shape = jax.ShapeDtypeStruct((QUAD**2 * (part + PARTS), size), BF16)

    def swap(sent, groups):
        return lax.all_to_all(sent, "seq", 0, 0, tiled=True, axis_index_groups=groups)

    def swap_states(states, groups):
        return swap(states.reshape(len(groups[0]), -1, 2, size), groups).reshape(states.shape)

    with jax.named_scope("summaries"):
        payload = pl.pallas_call(
            summary_kernel,
            in_specs=[in_hbm] * 3,
            out_specs=in_vmem,
            out_shape=state_shape,
            scratch_shapes=[
                pltpu.VMEM((heads, tokens), F32),
                pltpu.VMEM((tokens, features), BF16),
                pltpu.VMEM((tokens, features), BF16),
                pltpu.SemaphoreType.DMA((3,)),
            ],
            cost_estimate=pl.CostEstimate(flops=2 * heads * tokens * size * size, bytes_accessed=4 * tokens * features, transcendentals=0),
        )(rates, keys, values)
    block_states = swap_states(payload, near_groups())
    with jax.named_scope("group_totals"):
        group_totals = pl.pallas_call(
            total_kernel, in_specs=[in_vmem], out_specs=in_vmem, out_shape=state_shape, compiler_params=params
        )(block_states)
    group_states = swap_states(group_totals, far_groups())
    block_states, late_rates = lax.optimization_barrier((block_states, rates))
    with jax.named_scope("within"):
        parts, my_gain, my_place = pl.pallas_call(
            functools.partial(within_kernel, 256),
            in_specs=[in_smem] + [in_vmem] * 5,
            out_specs=[in_vmem] * 2 + [in_smem],
            out_shape=[
                jax.ShapeDtypeStruct((2, tokens, features), BF16),
                jax.ShapeDtypeStruct((heads, size), F32),
                jax.ShapeDtypeStruct((1,), jnp.int32),
            ],
            scratch_shapes=[pltpu.VMEM((tokens, size), F32)],
            compiler_params=pltpu.CompilerParams(vmem_limit_bytes=LARGE_VMEM),
            cost_estimate=pl.CostEstimate(
                flops=3 * heads * tokens * tokens * size, bytes_accessed=12 * tokens * features, transcendentals=heads * tokens * tokens
            ),
        )(place, gain.reshape(-1, size), late_rates, queries, keys, values)
    group_states, parts, my_gain, my_place = lax.optimization_barrier((group_states, parts, my_gain, my_place))
    with jax.named_scope("carry"):
        before = pl.pallas_call(
            carry_kernel,
            in_specs=[in_smem] + [in_vmem] * 2,
            out_specs=in_vmem,
            out_shape=jax.ShapeDtypeStruct((QUAD**2, part, size), BF16),
            compiler_params=params,
        )(my_place, group_states, block_states)
    incoming = swap(before, near_groups()).reshape(heads, size, size)
    with jax.named_scope("finish"):
        normed = pl.pallas_call(
            functools.partial(finish_kernel, 256, FIRST_HEAD * (tokens // owners)),
            in_specs=[in_vmem] * 3,
            out_specs=in_vmem,
            out_shape=jax.ShapeDtypeStruct((tokens, features), BF16),
            compiler_params=params,
        )(parts, incoming, my_gain)
    sent = normed.reshape(owners, tokens // owners, features)
    head_order = [(n + FIRST_HEAD) % owners for n in range(owners)]
    got = lax.all_to_all(sent, "head", 0, 0, tiled=True, axis_index_groups=[head_order])
    with jax.named_scope("lay_out"):
        return pl.pallas_call(
            functools.partial(lay_out_kernel, FIRST_HEAD),
            in_specs=[in_vmem],
            out_specs=in_hbm,
            out_shape=jax.ShapeDtypeStruct((tokens // owners, owners * features), BF16),
            scratch_shapes=[pltpu.SemaphoreType.DMA((owners,))],
            compiler_params=params,
        )(got)


def solution(mesh):
    placed = (P("seq", "head"), P("seq", "head"), P("seq", "head"), P("seq", "head"), P())
    return jax.shard_map(
        per_device, mesh=mesh, in_specs=placed, out_specs=P(("seq", "head"), None), check_vma=False
    )
```

```python
import functools
import math

import jax
import jax.numpy as jnp
from jax import lax
from jax.experimental import pallas as pl
from jax.experimental.pallas import tpu as pltpu
from jax.sharding import PartitionSpec as P

LANE = 128
F32 = jnp.float32
BF16 = jnp.bfloat16
PARTS = 2
QUAD = 4
NEAR = [1, 2, 3, 0]
FAR = [2, 3, 1, 0]
ROWS = [2, 3, 1, 0]
FIRST_HEAD = 4
LOG2_E = 1.4426950408889634
SMALL_VMEM = 16 * 1024 * 1024
LARGE_VMEM = 40 * 1024 * 1024


def split_three(x):
    high = x.astype(BF16)
    rest = x - high.astype(F32)
    middle = rest.astype(BF16)
    low = (rest - middle.astype(F32)).astype(BF16)
    return high, middle, low


def chunk_sums(rates, after):
    heads, tokens = rates.shape
    count = tokens // LANE
    rows = jnp.concatenate([rates[:, n * LANE : (n + 1) * LANE] for n in range(count)], axis=0)
    source = lax.broadcasted_iota(jnp.int32, (LANE, LANE), 0)
    target = lax.broadcasted_iota(jnp.int32, (LANE, LANE), 1)
    picked = (source > target) if after else (source <= target)
    picked = jnp.where(picked, 1.0, 0.0).astype(BF16)
    sums = sum(jnp.dot(part, picked, preferred_element_type=F32) for part in split_three(rows))
    if after:
        totals = sums[:, :1] + rows[:, :1]
    else:
        totals = sums[:, LANE - 1 :]
    running = jnp.zeros((heads, 1), F32)
    pieces = [None] * count
    for n in reversed(range(count)) if after else range(count):
        at = slice(n * heads, (n + 1) * heads)
        pieces[n] = sums[at] + running
        running = running + totals[at]
    return pieces, running


def pack_states(states):
    rows = []
    for state, keep in states:
        rows += [state] + [p.astype(F32) for p in split_three(keep)[:PARTS]]
    return jnp.concatenate(rows, axis=0).astype(BF16)


def unpack_states(ref):
    half = ref.shape[0] // 2
    slot = ref.shape[0] // QUAD**2
    states = []
    for first in (0, half):
        rows = ref[first : first + half, :].astype(F32)
        for at in range(0, half, slot):
            keep = rows[at + slot - 2 : at + slot - 1] + rows[at + slot - 1 : at + slot]
            states.append((rows[at : at + slot - PARTS], keep))
    return states


def summary_kernel(rate_hbm, key_hbm, value_hbm, out_ref, rates_ref, key_ref, value_ref, sems):
    heads, tokens = rates_ref.shape
    size = key_ref.shape[1] // heads
    copies = [
        pltpu.make_async_copy(source, target, sems.at[n])
        for n, (source, target) in enumerate(
            ((rate_hbm, rates_ref), (key_hbm, key_ref), (value_hbm, value_ref))
        )
    ]
    for copy in copies:
        copy.start()
    copies[0].wait()
    later, totals = chunk_sums(rates_ref[...], after=True)
    decays = jnp.exp(-jnp.concatenate(later, axis=1))
    keeps = jnp.exp(-totals)
    copies[1].wait()
    decayed_keys = []
    for h in range(heads):
        key_t = key_ref[:, h * size : (h + 1) * size].T
        decayed_keys.append((key_t.astype(F32) * decays[h : h + 1]).astype(BF16))
    copies[2].wait()
    states = []
    for h in range(heads):
        summary = jnp.dot(decayed_keys[h], value_ref[:, h * size : (h + 1) * size], preferred_element_type=F32)
        scales = (jnp.max(jnp.abs(summary), axis=1, keepdims=True) + 1e-06).astype(BF16).astype(F32)
        codes = (summary / scales).astype(BF16)
        restored = codes.astype(F32) * scales
        keep = jnp.broadcast_to(keeps[h : h + 1], (1, LANE))
        part = heads * size // QUAD**2
        states += [(restored[n : n + part], keep) for n in range(0, size, part)]
    half = out_ref.shape[0] // 2
    for n in range(2):
        out_ref[n * half : (n + 1) * half, :] = pack_states(states[n * len(states) // 2 : (n + 1) * len(states) // 2])


def slot_of(row, near):
    return ROWS.index(row) * QUAD + NEAR.index(near)


def total_kernel(in_ref, out_ref):
    blocks = unpack_states(in_ref)
    totals = []
    for row in range(QUAD):
        state, keep = blocks[slot_of(row, 0)]
        for near in range(1, QUAD):
            more, more_keep = blocks[slot_of(row, near)]
            state = state * more_keep + more
            keep = keep * more_keep
        totals.append((state, keep))
    packed = pack_states(totals + totals)
    half = out_ref.shape[0] // 2
    for n in range(2):
        out_ref[n * half : (n + 1) * half, :] = packed


def carry_kernel(place_ref, groups_ref, blocks_ref, out_ref):
    groups, blocks = unpack_states(groups_ref), unpack_states(blocks_ref)
    mine = place_ref[0] // QUAD % QUAD
    carry = jnp.zeros(out_ref.shape[1:], F32)
    for row in range(QUAD):
        start = carry
        for far in range(QUAD):
            start = jnp.where(mine == far, carry, start)
            state, keep = groups[FAR.index(far) * QUAD + row]
            carry = carry * keep + state
        for near in range(QUAD):
            slot = slot_of(row, near)
            out_ref[slot] = start.astype(BF16)
            state, keep = blocks[slot]
            start = start * keep + state


def within_kernel(
    span,
    place_ref,
    gain_ref,
    rates_ref,
    query_ref,
    key_ref,
    value_ref,
    parts_ref,
    gain_out_ref,
    place_out_ref,
):
    heads, tokens = rates_ref.shape
    size = query_ref.shape[1] // heads
    place_out_ref[0] = place_ref[1]
    for h in range(heads):
        gain_out_ref[h : h + 1] = gain_ref[pl.ds(place_ref[0] * heads + h, 1), :]
    upto, _ = chunk_sums(rates_ref[...], after=False)
    count = len(upto)
    stacked = -jnp.concatenate(upto, axis=0) * LOG2_E
    columns = jnp.concatenate([stacked] * (LANE // (count * heads)), axis=0).T
    place_t = lax.broadcasted_iota(jnp.int32, (span, span), 0)
    place_s = lax.broadcasted_iota(jnp.int32, (span, span), 1)
    for h in range(heads):
        at_h = slice(h * size, (h + 1) * size)
        places = [n * heads + h for n in range(count)]
        column = jnp.concatenate([columns[:, n : n + 1] for n in places], axis=0) - 0.5 * math.log2(size)
        row = jnp.concatenate([stacked[n : n + 1] for n in places], axis=1)
        parts_ref[0, :, at_h] = (query_ref[:, at_h].astype(F32) * jnp.exp2(column)).astype(BF16)
        state = None
        for first in range(0, tokens, span):
            at = slice(first, first + span)
            query, key, value = query_ref[at, at_h], key_ref[at, at_h], value_ref[at, at_h]
            scores = lax.dot_general(query, key, (((1,), (1,)), ((), ())), preferred_element_type=F32)
            spread = jnp.where(place_t >= place_s, column[at] - row[:, at], -jnp.inf)
            total = jnp.dot((scores * jnp.exp2(spread)).astype(BF16), value, preferred_element_type=F32)
            if first > 0:
                base = row[:, first - 1 : first]
                scaled = (query.astype(F32) * jnp.exp2(column[at] - base)).astype(BF16)
                total += jnp.dot(scaled, state.astype(BF16), preferred_element_type=F32)
            if first + span < tokens:
                end = row[:, first + span - 1 : first + span]
                decayed = (key.T.astype(F32) * jnp.exp2(end - row[:, at])).astype(BF16)
                added = jnp.dot(decayed, value, preferred_element_type=F32)
                state = added if first == 0 else state * jnp.exp2(end - base) + added
            parts_ref[1, at, at_h] = total.astype(BF16)


def finish_kernel(span, first_row, parts_ref, incoming_ref, gain_ref, out_ref):
    tokens = parts_ref.shape[1]
    heads, size, _ = incoming_ref.shape
    mean_of = jnp.full((size, size), 1.0 / size, BF16)
    for h in range(heads):
        columns = slice(h * size, (h + 1) * size)
        gain = gain_ref[h : h + 1]
        for first in range(0, tokens, span):
            at = slice(first, first + span)
            carried = jnp.dot(parts_ref[0, at, columns], incoming_ref[h], preferred_element_type=F32)
            retained = (parts_ref[1, at, columns].astype(F32) + carried).astype(BF16)
            center = jnp.dot(retained, mean_of, preferred_element_type=F32)
            deviation = retained.astype(F32) - center
            variance = jnp.sum(deviation * deviation, axis=1, keepdims=True) * (1.0 / size)
            to = (first - first_row) % tokens
            out_ref[to : to + span, columns] = (deviation * lax.rsqrt(variance + 1e-05) * gain).astype(BF16)


def lay_out_kernel(first, in_ref, out_hbm, sems):
    owners, _, features = in_ref.shape
    copies = []
    for n in range(owners):
        columns = pl.ds((n + first) % owners * features, features)
        copies.append(pltpu.make_async_copy(in_ref.at[n], out_hbm.at[:, columns], sems.at[n]))
    for copy in copies:
        copy.start()
    for copy in copies:
        copy.wait()


def near_groups():
    return [
        [(row * QUAD + far) * QUAD + near for row in ROWS for near in NEAR] for far in range(QUAD)
    ]


def far_groups():
    return [
        [(row * QUAD + far) * QUAD + near for far in FAR] for row in range(QUAD) for near in range(QUAD)
    ]


def per_device(queries, keys, values, decay_rate, gain):
    tokens, features = queries.shape
    heads = decay_rate.shape[1]
    size = features // heads
    blocks = lax.axis_size("seq")
    owners = lax.axis_size("head")
    rates = decay_rate.T
    params = pltpu.CompilerParams(vmem_limit_bytes=SMALL_VMEM)

    in_hbm = pl.BlockSpec(memory_space=pl.ANY)
    in_vmem = pl.BlockSpec(memory_space=pltpu.VMEM)
    in_smem = pl.BlockSpec(memory_space=pltpu.SMEM)
    place = jnp.stack([lax.axis_index("head"), lax.axis_index("seq")]).astype(jnp.int32)
    part = heads * size // QUAD**2
    state_shape = jax.ShapeDtypeStruct((QUAD**2 * (part + PARTS), size), BF16)

    def swap(sent, groups):
        return lax.all_to_all(sent, "seq", 0, 0, tiled=True, axis_index_groups=groups)

    def swap_states(states, groups):
        return swap(states.reshape(len(groups[0]), -1, 2, size), groups).reshape(states.shape)

    with jax.named_scope("summaries"):
        payload = pl.pallas_call(
            summary_kernel,
            in_specs=[in_hbm] * 3,
            out_specs=in_vmem,
            out_shape=state_shape,
            scratch_shapes=[
                pltpu.VMEM((heads, tokens), F32),
                pltpu.VMEM((tokens, features), BF16),
                pltpu.VMEM((tokens, features), BF16),
                pltpu.SemaphoreType.DMA((3,)),
            ],
            cost_estimate=pl.CostEstimate(flops=2 * heads * tokens * size * size, bytes_accessed=4 * tokens * features, transcendentals=0),
        )(rates, keys, values)
    block_states = swap_states(payload, near_groups())
    with jax.named_scope("group_totals"):
        group_totals = pl.pallas_call(
            total_kernel, in_specs=[in_vmem], out_specs=in_vmem, out_shape=state_shape, compiler_params=params
        )(block_states)
    group_states = swap_states(group_totals, far_groups())
    block_states, late_rates = lax.optimization_barrier((block_states, rates))
    with jax.named_scope("within"):
        parts, my_gain, my_place = pl.pallas_call(
            functools.partial(within_kernel, 256),
            in_specs=[in_smem] + [in_vmem] * 5,
            out_specs=[in_vmem] * 2 + [in_smem],
            out_shape=[
                jax.ShapeDtypeStruct((2, tokens, features), BF16),
                jax.ShapeDtypeStruct((heads, size), F32),
                jax.ShapeDtypeStruct((1,), jnp.int32),
            ],
            compiler_params=pltpu.CompilerParams(vmem_limit_bytes=LARGE_VMEM),
            cost_estimate=pl.CostEstimate(
                flops=3 * heads * tokens * tokens * size, bytes_accessed=12 * tokens * features, transcendentals=heads * tokens * tokens
            ),
        )(place, gain.reshape(-1, size), late_rates, queries, keys, values)
    group_states, parts, my_gain, my_place = lax.optimization_barrier((group_states, parts, my_gain, my_place))
    with jax.named_scope("carry"):
        before = pl.pallas_call(
            carry_kernel,
            in_specs=[in_smem] + [in_vmem] * 2,
            out_specs=in_vmem,
            out_shape=jax.ShapeDtypeStruct((QUAD**2, part, size), BF16),
            compiler_params=params,
        )(my_place, group_states, block_states)
    incoming = swap(before, near_groups()).reshape(heads, size, size)
    with jax.named_scope("finish"):
        normed = pl.pallas_call(
            functools.partial(finish_kernel, 256, FIRST_HEAD * (tokens // owners)),
            in_specs=[in_vmem] * 3,
            out_specs=in_vmem,
            out_shape=jax.ShapeDtypeStruct((tokens, features), BF16),
            compiler_params=params,
        )(parts, incoming, my_gain)
    sent = normed.reshape(owners, tokens // owners, features)
    head_order = [(n + FIRST_HEAD) % owners for n in range(owners)]
    got = lax.all_to_all(sent, "head", 0, 0, tiled=True, axis_index_groups=[head_order])
    with jax.named_scope("lay_out"):
        return pl.pallas_call(
            functools.partial(lay_out_kernel, FIRST_HEAD),
            in_specs=[in_vmem],
            out_specs=in_hbm,
            out_shape=jax.ShapeDtypeStruct((tokens // owners, owners * features), BF16),
            scratch_shapes=[pltpu.SemaphoreType.DMA((owners,))],
            compiler_params=params,
        )(got)


def solution(mesh):
    placed = (P("seq", "head"), P("seq", "head"), P("seq", "head"), P("seq", "head"), P())
    return jax.shard_map(
        per_device, mesh=mesh, in_specs=placed, out_specs=P(("seq", "head"), None), check_vma=False
    )
```

```python
import functools
import math

import jax
import jax.numpy as jnp
from jax import lax
from jax.experimental import pallas as pl
from jax.experimental.pallas import tpu as pltpu
from jax.sharding import PartitionSpec as P

LANE = 128
F32 = jnp.float32
BF16 = jnp.bfloat16
PARTS = 2
QUAD = 4
NEAR = [2, 1, 3, 0]
FAR = [2, 3, 1, 0]
ROWS = [2, 3, 1, 0]
FIRST_HEAD = 4
LOG2_E = 1.4426950408889634
SMALL_VMEM = 16 * 1024 * 1024
LARGE_VMEM = 40 * 1024 * 1024


def split_three(x):
    high = x.astype(BF16)
    rest = x - high.astype(F32)
    middle = rest.astype(BF16)
    low = (rest - middle.astype(F32)).astype(BF16)
    return high, middle, low


def chunk_sums(rates, after):
    heads, tokens = rates.shape
    count = tokens // LANE
    rows = jnp.concatenate([rates[:, n * LANE : (n + 1) * LANE] for n in range(count)], axis=0)
    source = lax.broadcasted_iota(jnp.int32, (LANE, LANE), 0)
    target = lax.broadcasted_iota(jnp.int32, (LANE, LANE), 1)
    picked = (source > target) if after else (source <= target)
    picked = jnp.where(picked, 1.0, 0.0).astype(BF16)
    sums = sum(jnp.dot(part, picked, preferred_element_type=F32) for part in split_three(rows))
    if after:
        totals = sums[:, :1] + rows[:, :1]
    else:
        totals = sums[:, LANE - 1 :]
    running = jnp.zeros((heads, 1), F32)
    pieces = [None] * count
    for n in reversed(range(count)) if after else range(count):
        at = slice(n * heads, (n + 1) * heads)
        pieces[n] = sums[at] + running
        running = running + totals[at]
    return pieces, running


def pack_states(states):
    rows = []
    for state, keep in states:
        rows += [state] + [p.astype(F32) for p in split_three(keep)[:PARTS]]
    return jnp.concatenate(rows, axis=0).astype(BF16)


def unpack_states(ref):
    half = ref.shape[0] // 2
    slot = ref.shape[0] // QUAD**2
    states = []
    for first in (0, half):
        rows = ref[first : first + half, :].astype(F32)
        for at in range(0, half, slot):
            keep = rows[at + slot - 2 : at + slot - 1] + rows[at + slot - 1 : at + slot]
            states.append((rows[at : at + slot - PARTS], keep))
    return states


def summary_kernel(rate_hbm, key_hbm, value_hbm, out_ref, rates_ref, key_ref, value_ref, sems):
    heads, tokens = rates_ref.shape
    size = key_ref.shape[1] // heads
    copies = [
        pltpu.make_async_copy(source, target, sems.at[n])
        for n, (source, target) in enumerate(
            ((rate_hbm, rates_ref), (key_hbm, key_ref), (value_hbm, value_ref))
        )
    ]
    for copy in copies:
        copy.start()
    copies[0].wait()
    later, totals = chunk_sums(rates_ref[...], after=True)
    decays = jnp.exp(-jnp.concatenate(later, axis=1))
    keeps = jnp.exp(-totals)
    copies[1].wait()
    decayed_keys = []
    for h in range(heads):
        key_t = key_ref[:, h * size : (h + 1) * size].T
        decayed_keys.append((key_t.astype(F32) * decays[h : h + 1]).astype(BF16))
    copies[2].wait()
    states = []
    for h in range(heads):
        summary = jnp.dot(decayed_keys[h], value_ref[:, h * size : (h + 1) * size], preferred_element_type=F32)
        scales = (jnp.max(jnp.abs(summary), axis=1, keepdims=True) + 1e-06).astype(BF16).astype(F32)
        codes = (summary / scales).astype(BF16)
        restored = codes.astype(F32) * scales
        keep = jnp.broadcast_to(keeps[h : h + 1], (1, LANE))
        part = heads * size // QUAD**2
        states += [(restored[n : n + part], keep) for n in range(0, size, part)]
    half = out_ref.shape[0] // 2
    for n in range(2):
        out_ref[n * half : (n + 1) * half, :] = pack_states(states[n * len(states) // 2 : (n + 1) * len(states) // 2])


def slot_of(row, near):
    return ROWS.index(row) * QUAD + NEAR.index(near)


def total_kernel(in_ref, out_ref):
    blocks = unpack_states(in_ref)
    totals = []
    for row in range(QUAD):
        state, keep = blocks[slot_of(row, 0)]
        for near in range(1, QUAD):
            more, more_keep = blocks[slot_of(row, near)]
            state = state * more_keep + more
            keep = keep * more_keep
        totals.append((state, keep))
    packed = pack_states(totals + totals)
    half = out_ref.shape[0] // 2
    for n in range(2):
        out_ref[n * half : (n + 1) * half, :] = packed


def carry_kernel(place_ref, groups_ref, blocks_ref, out_ref):
    groups, blocks = unpack_states(groups_ref), unpack_states(blocks_ref)
    mine = place_ref[0] // QUAD % QUAD
    carry = jnp.zeros(out_ref.shape[1:], F32)
    for row in range(QUAD):
        start = carry
        for far in range(QUAD):
            start = jnp.where(mine == far, carry, start)
            state, keep = groups[FAR.index(far) * QUAD + row]
            carry = carry * keep + state
        for near in range(QUAD):
            slot = slot_of(row, near)
            out_ref[slot] = start.astype(BF16)
            state, keep = blocks[slot]
            start = start * keep + state


def within_kernel(
    span,
    place_ref,
    gain_ref,
    rates_ref,
    query_ref,
    key_ref,
    value_ref,
    parts_ref,
    gain_out_ref,
    place_out_ref,
):
    heads, tokens = rates_ref.shape
    size = query_ref.shape[1] // heads
    place_out_ref[0] = place_ref[1]
    for h in range(heads):
        gain_out_ref[h : h + 1] = gain_ref[pl.ds(place_ref[0] * heads + h, 1), :]
    upto, _ = chunk_sums(rates_ref[...], after=False)
    count = len(upto)
    stacked = -jnp.concatenate(upto, axis=0) * LOG2_E
    columns = jnp.concatenate([stacked] * (LANE // (count * heads)), axis=0).T
    place_t = lax.broadcasted_iota(jnp.int32, (span, span), 0)
    place_s = lax.broadcasted_iota(jnp.int32, (span, span), 1)
    for h in range(heads):
        at_h = slice(h * size, (h + 1) * size)
        places = [n * heads + h for n in range(count)]
        column = jnp.concatenate([columns[:, n : n + 1] for n in places], axis=0) - 0.5 * math.log2(size)
        row = jnp.concatenate([stacked[n : n + 1] for n in places], axis=1)
        parts_ref[0, :, at_h] = (query_ref[:, at_h].astype(F32) * jnp.exp2(column)).astype(BF16)
        state = None
        for first in range(0, tokens, span):
            at = slice(first, first + span)
            query, key, value = query_ref[at, at_h], key_ref[at, at_h], value_ref[at, at_h]
            scores = lax.dot_general(query, key, (((1,), (1,)), ((), ())), preferred_element_type=F32)
            spread = jnp.where(place_t >= place_s, column[at] - row[:, at], -jnp.inf)
            total = jnp.dot((scores * jnp.exp2(spread)).astype(BF16), value, preferred_element_type=F32)
            if first > 0:
                base = row[:, first - 1 : first]
                scaled = (query.astype(F32) * jnp.exp2(column[at] - base)).astype(BF16)
                total += jnp.dot(scaled, state.astype(BF16), preferred_element_type=F32)
            if first + span < tokens:
                end = row[:, first + span - 1 : first + span]
                decayed = (key.T.astype(F32) * jnp.exp2(end - row[:, at])).astype(BF16)
                added = jnp.dot(decayed, value, preferred_element_type=F32)
                state = added if first == 0 else state * jnp.exp2(end - base) + added
            parts_ref[1, at, at_h] = total.astype(BF16)


def finish_kernel(span, first_row, parts_ref, incoming_ref, gain_ref, out_ref):
    tokens = parts_ref.shape[1]
    heads, size, _ = incoming_ref.shape
    mean_of = jnp.full((size, size), 1.0 / size, BF16)
    for h in range(heads):
        columns = slice(h * size, (h + 1) * size)
        gain = gain_ref[h : h + 1]
        for first in range(0, tokens, span):
            at = slice(first, first + span)
            carried = jnp.dot(parts_ref[0, at, columns], incoming_ref[h], preferred_element_type=F32)
            retained = (parts_ref[1, at, columns].astype(F32) + carried).astype(BF16)
            center = jnp.dot(retained, mean_of, preferred_element_type=F32)
            deviation = retained.astype(F32) - center
            variance = jnp.sum(deviation * deviation, axis=1, keepdims=True) * (1.0 / size)
            to = (first - first_row) % tokens
            out_ref[to : to + span, columns] = (deviation * lax.rsqrt(variance + 1e-05) * gain).astype(BF16)


def lay_out_kernel(first, in_ref, out_hbm, sems):
    owners, _, features = in_ref.shape
    copies = []
    for n in range(owners):
        columns = pl.ds((n + first) % owners * features, features)
        copies.append(pltpu.make_async_copy(in_ref.at[n], out_hbm.at[:, columns], sems.at[n]))
    for copy in copies:
        copy.start()
    for copy in copies:
        copy.wait()


def near_groups():
    return [
        [(row * QUAD + far) * QUAD + near for row in ROWS for near in NEAR] for far in range(QUAD)
    ]


def far_groups():
    return [
        [(row * QUAD + far) * QUAD + near for far in FAR] for row in range(QUAD) for near in range(QUAD)
    ]


def per_device(queries, keys, values, decay_rate, gain):
    tokens, features = queries.shape
    heads = decay_rate.shape[1]
    size = features // heads
    blocks = lax.axis_size("seq")
    owners = lax.axis_size("head")
    rates = decay_rate.T
    params = pltpu.CompilerParams(vmem_limit_bytes=SMALL_VMEM)

    in_hbm = pl.BlockSpec(memory_space=pl.ANY)
    in_vmem = pl.BlockSpec(memory_space=pltpu.VMEM)
    in_smem = pl.BlockSpec(memory_space=pltpu.SMEM)
    place = jnp.stack([lax.axis_index("head"), lax.axis_index("seq")]).astype(jnp.int32)
    part = heads * size // QUAD**2
    state_shape = jax.ShapeDtypeStruct((QUAD**2 * (part + PARTS), size), BF16)

    def swap(sent, groups):
        return lax.all_to_all(sent, "seq", 0, 0, tiled=True, axis_index_groups=groups)

    def swap_states(states, groups):
        return swap(states.reshape(len(groups[0]), -1, 2, size), groups).reshape(states.shape)

    with jax.named_scope("summaries"):
        payload = pl.pallas_call(
            summary_kernel,
            in_specs=[in_hbm] * 3,
            out_specs=in_vmem,
            out_shape=state_shape,
            scratch_shapes=[
                pltpu.VMEM((heads, tokens), F32),
                pltpu.VMEM((tokens, features), BF16),
                pltpu.VMEM((tokens, features), BF16),
                pltpu.SemaphoreType.DMA((3,)),
            ],
            cost_estimate=pl.CostEstimate(flops=2 * heads * tokens * size * size, bytes_accessed=4 * tokens * features, transcendentals=0),
        )(rates, keys, values)
    block_states = swap_states(payload, near_groups())
    with jax.named_scope("group_totals"):
        group_totals = pl.pallas_call(
            total_kernel, in_specs=[in_vmem], out_specs=in_vmem, out_shape=state_shape, compiler_params=params
        )(block_states)
    group_states = swap_states(group_totals, far_groups())
    block_states, late_rates = lax.optimization_barrier((block_states, rates))
    with jax.named_scope("within"):
        parts, my_gain, my_place = pl.pallas_call(
            functools.partial(within_kernel, 256),
            in_specs=[in_smem] + [in_vmem] * 5,
            out_specs=[in_vmem] * 2 + [in_smem],
            out_shape=[
                jax.ShapeDtypeStruct((2, tokens, features), BF16),
                jax.ShapeDtypeStruct((heads, size), F32),
                jax.ShapeDtypeStruct((1,), jnp.int32),
            ],
            compiler_params=pltpu.CompilerParams(vmem_limit_bytes=LARGE_VMEM),
            cost_estimate=pl.CostEstimate(
                flops=3 * heads * tokens * tokens * size, bytes_accessed=12 * tokens * features, transcendentals=heads * tokens * tokens
            ),
        )(place, gain.reshape(-1, size), late_rates, queries, keys, values)
    group_states, parts, my_gain, my_place = lax.optimization_barrier((group_states, parts, my_gain, my_place))
    with jax.named_scope("carry"):
        before = pl.pallas_call(
            carry_kernel,
            in_specs=[in_smem] + [in_vmem] * 2,
            out_specs=in_vmem,
            out_shape=jax.ShapeDtypeStruct((QUAD**2, part, size), BF16),
            compiler_params=params,
        )(my_place, group_states, block_states)
    incoming = swap(before, near_groups()).reshape(heads, size, size)
    with jax.named_scope("finish"):
        normed = pl.pallas_call(
            functools.partial(finish_kernel, 256, FIRST_HEAD * (tokens // owners)),
            in_specs=[in_vmem] * 3,
            out_specs=in_vmem,
            out_shape=jax.ShapeDtypeStruct((tokens, features), BF16),
            compiler_params=params,
        )(parts, incoming, my_gain)
    sent = normed.reshape(owners, tokens // owners, features)
    head_order = [(n + FIRST_HEAD) % owners for n in range(owners)]
    got = lax.all_to_all(sent, "head", 0, 0, tiled=True, axis_index_groups=[head_order])
    with jax.named_scope("lay_out"):
        return pl.pallas_call(
            functools.partial(lay_out_kernel, FIRST_HEAD),
            in_specs=[in_vmem],
            out_specs=in_hbm,
            out_shape=jax.ShapeDtypeStruct((tokens // owners, owners * features), BF16),
            scratch_shapes=[pltpu.SemaphoreType.DMA((owners,))],
            compiler_params=params,
        )(got)


def solution(mesh):
    placed = (P("seq", "head"), P("seq", "head"), P("seq", "head"), P("seq", "head"), P())
    return jax.shard_map(
        per_device, mesh=mesh, in_specs=placed, out_specs=P(("seq", "head"), None), check_vma=False
    )
```
